512 devices in a mesh: dom: 64 (over y, x, z_lo), rel: 8 (over z_hi, core).
Axes of the slice: x: 4, y: 8, z: 8 (z_hi: 4, z_lo: 2; z = z_hi * 2 + z_lo), core: 2. Of those that a mesh axis runs over, the one named last changes fastest.
Arguments:
- embeddings: bfloat16 [65536, 256], P(('dom', 'rel')), may hold values from -4 to 4
- relations: float32 [8192, 256], P('rel'), may hold values from -6 to 6
- lhs_ids: int32 [64, 8, 512], P('dom', 'rel'), may hold values from 0 to 1023
- rhs_ids: int32 [64, 8, 512], P('dom', 'rel'), may hold values from 0 to 1023
- rel_ids: int32 [64, 8, 512], P('dom', 'rel'), may hold values from 0 to 1023
- neg_ids: int32 [64, 8, 1, 2048], P('dom', 'rel'), may hold values from 0 to 1023
- live: int32 [512], P(('dom', 'rel')), may hold values from 1 to 512, 131072 in all
Outputs:
- entity_grad: float32 [65536, 256], P(('dom', 'rel'))
- relation_grad: float32 [8192, 256], P('rel')
The draws below stay inside these ranges and needn't reach their ends.
Inputs may be any that keep to these rules, and one draw needn't show every extreme that they name: Slots of a device below its live count hold its live edges; the others add nothing.
All inputs are finite; a program needn't handle non-finite values.
Results may differ from the reference program's by a relative error of at most 0.009.
Values may be sent and summed in bfloat16 or wider, within the bound.
No kernel may reach another device: no remote copies, remote signals or barrier semaphores. Data moves between devices by JAX's collectives and lax.ppermute only.
A program may use at most 64 MiB of HBM per device.

```python
import math
import jax
import jax.numpy as jnp
import numpy as np
from jax import lax

D = 256
NEG = 2048
BLOCKS = 1
ENT_DEV = 128
REL_DEV = 1024
EDGE_DEV = 512
ENT_PART = 1024
ENTITIES = 65536
RELATIONS = 8192
N_DOM = 64
N_REL = 8


def plant(drawn, stream_key, smallest, top_value):
    longest = drawn.shape.index(max(drawn.shape))
    spots = []
    for shift in (0, 1):
        where = [jax.random.randint(jax.random.fold_in(stream_key, axis), (), 0, length) for axis, length in enumerate(drawn.shape)]
        where[longest] = (where[longest] + shift) % drawn.shape[longest]
        spots.append(tuple(where))
    return drawn.at[spots[0]].set(smallest).at[spots[1]].set(top_value)


def steps_of(stream_key, shape, split, least, top_value):
    level, own = 1.0, jax.random.fold_in(stream_key, 6)
    for dim, blocks in split:
        draws = jnp.exp(jax.random.uniform(jax.random.fold_in(own, dim), (blocks,), jnp.float32, least / len(split), top_value / len(split)))
        level = level * jnp.repeat(draws, shape[dim] // blocks).reshape([-1 if axis == dim else 1 for axis in range(len(shape))])
    return level


def length_profile(amount, total, limit, lean):
    weights = [(1 << 20) // math.isqrt(rank ** lean) + 1 for rank in range(2, amount + 1)]
    rest, given = total - limit - (amount - 1), [1] * (amount - 1)
    while rest > 0:
        movable = [i for i in range(amount - 1) if given[i] < limit]
        pool, budget = sum([weights[i] for i in movable]), rest
        for i in movable:
            addition = min(limit - given[i], max(1, budget * weights[i] // pool), rest)
            given[i] = given[i] + addition
            rest = rest - addition
    return np.array([limit] + given)


def ragged_sizes(stream_key, count, total, bound, slope):
    if count == 2:
        one = jax.random.randint(stream_key, (), max(1, total - bound), min(bound, total - 1) + 1)
        return jnp.stack([one, total - one])
    sizes = jnp.asarray(length_profile(count, total, bound, slope), jnp.int32)
    pairs = (count - 1) // 2
    giver, sink = sizes[1:1 + 2 * pairs:2], sizes[2:2 + 2 * pairs:2]
    room = jnp.minimum(giver - 1, bound - sink)
    shifted = jax.random.randint(jax.random.fold_in(stream_key, 1), (pairs,), 0, 1 << 20) % (room + 1)
    sizes = sizes.at[1:1 + 2 * pairs:2].set(giver - shifted).at[2:2 + 2 * pairs:2].set(sink + shifted)
    return sizes[jax.random.permutation(jax.random.fold_in(stream_key, 2), count)]


def normal_values(own_key, extent, scale, most, cuts=(), kind=jnp.bfloat16):
    result = scale * jax.random.normal(own_key, extent, jnp.float32)
    if cuts:
        result = result * steps_of(own_key, extent, cuts, -0.22, 0.18)
    return jnp.clip(result, -most, most).astype(kind)


def setup_inputs(seed: int = 0) -> dict:
    key_list = jax.random.split(jax.random.key(seed), 8)
    return {
        "embeddings": normal_values(key_list[0], (ENTITIES, D), 0.25, 4.0, ((0, 512),)),
        "relations": normal_values(key_list[1], (RELATIONS, D), 1.0, 6.0, ((0, 8),), jnp.float32),
        "lhs_ids": plant(jax.random.randint(key_list[2], (N_DOM, N_REL, EDGE_DEV), 0, ENT_PART), jax.random.fold_in(key_list[2], 1), 0, ENT_PART - 1).astype(jnp.int32),
        "rhs_ids": plant(jax.random.randint(key_list[3], (N_DOM, N_REL, EDGE_DEV), 0, ENT_PART), jax.random.fold_in(key_list[3], 1), 0, ENT_PART - 1).astype(jnp.int32),
        "rel_ids": plant(jax.random.randint(key_list[4], (N_DOM, N_REL, EDGE_DEV), 0, REL_DEV), jax.random.fold_in(key_list[4], 1), 0, REL_DEV - 1).astype(jnp.int32),
        "neg_ids": plant(jax.random.randint(key_list[5], (N_DOM, N_REL, BLOCKS, NEG), 0, ENT_PART), jax.random.fold_in(key_list[5], 1), 0, ENT_PART - 1).astype(jnp.int32),
        "live": ragged_sizes(key_list[6], N_DOM * N_REL, N_DOM * N_REL * EDGE_DEV // 2, EDGE_DEV, 2).astype(jnp.int32),
    }


def complex_split(values):
    width = values.shape[-1] // 2
    return values[..., :width], values[..., width:]


def edge_terms(own_block, partner_block, rel_table, lhs_index, rhs_index, rel_index, neg_index, live_count):
    edge_count = lhs_index.shape[0]
    blocks, negatives = neg_index.shape
    block_rows = edge_count // blocks
    weight = negatives ** -0.5
    alive_mask = (jnp.arange(edge_count) < live_count).astype(jnp.float32)
    head_rows = own_block[lhs_index].astype(jnp.float32)
    tail_rows = partner_block[rhs_index].astype(jnp.float32)
    rel_rows = rel_table[rel_index].astype(jnp.float32)
    head_real, head_imag = complex_split(head_rows)
    rel_real, rel_imag = complex_split(rel_rows)
    query_vec = jnp.concatenate([head_real * rel_real - head_imag * rel_imag,
                                 head_real * rel_imag + head_imag * rel_real], axis=-1).astype(jnp.bfloat16)
    query_wide = query_vec.astype(jnp.float32)
    pos_score = jnp.sum(query_wide * tail_rows, axis=-1)
    pos_grad = -jax.nn.sigmoid(-pos_score) * alive_mask
    partner_grad = jnp.zeros(partner_block.shape, jnp.float32).at[rhs_index].add(pos_grad[:, None] * query_wide)
    neg_parts = []
    for block_id in range(blocks):
        rows_here = query_vec[block_id * block_rows:(block_id + 1) * block_rows]
        neg_rows = partner_block[neg_index[block_id]]
        scores = lax.dot_general(rows_here, neg_rows, (((1,), (1,)), ((), ())), preferred_element_type=jnp.float32)
        mask_here = alive_mask[block_id * block_rows:(block_id + 1) * block_rows]
        neg_grad = (jax.nn.sigmoid(scores) * (weight * mask_here)[:, None]).astype(jnp.bfloat16)
        neg_parts.append(jnp.dot(neg_grad, neg_rows, preferred_element_type=jnp.float32))
        row_grad = lax.dot_general(neg_grad, rows_here, (((0,), (0,)), ((), ())), preferred_element_type=jnp.float32)
        partner_grad = partner_grad.at[neg_index[block_id]].add(row_grad)
    query_grad = pos_grad[:, None] * tail_rows + jnp.concatenate(neg_parts, axis=0)
    grad_real, grad_imag = complex_split(query_grad)
    head_grad = jnp.concatenate([grad_real * rel_real + grad_imag * rel_imag,
                                 grad_imag * rel_real - grad_real * rel_imag], axis=-1)
    rel_term = jnp.concatenate([grad_real * head_real + grad_imag * head_imag,
                                grad_imag * head_real - grad_real * head_imag], axis=-1)
    own_grad = jnp.zeros(own_block.shape, jnp.float32).at[lhs_index].add(head_grad)
    rel_partial = jnp.zeros(rel_table.shape, jnp.float32).at[rel_index].add(rel_term)
    return own_grad, partner_grad, rel_partial


def reference(embeddings, relations, lhs_ids, rhs_ids, rel_ids, neg_ids, live):
    part_rows = ENT_DEV * N_REL
    parts = embeddings.reshape(N_DOM, part_rows, D)
    rel_shards = relations.reshape(N_REL, REL_DEV, D)
    live_grid = live.reshape(N_DOM, N_REL)
    half_way = N_DOM // 2

    def visit(device, carry):
        ent_acc, rel_acc = carry
        dom_pos = (device // N_REL).astype(jnp.int32)
        rel_pos = (device % N_REL).astype(jnp.int32)
        partner_pos = ((dom_pos + N_DOM - half_way) % N_DOM).astype(jnp.int32)
        own_grad, partner_grad, rel_partial = edge_terms(
            parts[dom_pos], parts[partner_pos], rel_shards[rel_pos],
            lhs_ids[dom_pos, rel_pos], rhs_ids[dom_pos, rel_pos], rel_ids[dom_pos, rel_pos],
            neg_ids[dom_pos, rel_pos], live_grid[dom_pos, rel_pos])
        own_round = lax.optimization_barrier(own_grad.astype(jnp.bfloat16))
        partner_round = lax.optimization_barrier(partner_grad.astype(jnp.bfloat16))
        ent_acc = ent_acc.at[dom_pos].add(own_round.astype(jnp.float32))
        ent_acc = ent_acc.at[partner_pos].add(partner_round.astype(jnp.float32))
        rel_acc = rel_acc.at[rel_pos].add(rel_partial)
        return ent_acc, rel_acc

    start = (jnp.zeros((N_DOM, part_rows, D), jnp.float32), jnp.zeros((N_REL, REL_DEV, D), jnp.float32))
    ent_acc, rel_acc = lax.fori_loop(0, N_DOM * N_REL, visit, start)
    return ent_acc.reshape(N_DOM * part_rows, D), rel_acc.reshape(N_REL * REL_DEV, D)
```

```python
import jax
import jax.numpy as jnp
from jax import lax
from jax.experimental import pallas as pl
from jax.experimental.pallas import tpu as pltpu
from jax.sharding import Mesh
from jax.sharding import PartitionSpec as P

F32 = jnp.float32
BF16 = jnp.bfloat16
AXES = ("yh", "yl", "x", "zl", "zh", "core")
Y = ("yh", "yl")
XZ = ("x", "zl")

D = 256
HALF = 128
SHARD = 128
EDGES = 512
CHUNK = 256
PARTS = 1024


def dot(a, b, ca, cb):
    return lax.dot_general(a, b, (((ca,), (cb,)), ((), ())), preferred_element_type=F32)


def edge_kernel(
    scal_ref, lhs_ref, rhs_ref, rel_ref, neg_ref, mine_ref, other_ref, table_ref,
    mine_out, other_out, rel_out,
    counts,
):
    live, core = scal_ref[0], scal_ref[1]
    weight = neg_ref.shape[1] ** (-0.5)

    def place(ids):
        owner = jnp.bitwise_and(jnp.right_shift(ids, 7), 1)
        slot = jnp.right_shift(ids, 8)
        side = jnp.where(owner == core, 0, 512)
        return side + slot * SHARD + jnp.bitwise_and(ids, SHARD - 1)

    def chunk_of(ref_a, ref_b, part, step):
        ref = ref_a if step < 2 else ref_b
        s = 2 * (step % 2)
        return jnp.concatenate(
            [ref[s, part * SHARD:(part + 1) * SHARD], ref[s + 1, part * SHARD:(part + 1) * SHARD]], axis=0
        )

    lhs = place(lhs_ref[...])
    rhs = place(rhs_ref[...])
    rel = rel_ref[...]
    neg = place(neg_ref[...])
    alive = (lax.broadcasted_iota(jnp.int32, (1, EDGES), 1) < live).astype(F32)
    rows = lax.broadcasted_iota(jnp.int32, (CHUNK, EDGES), 0)

    def one_hot(ids, step):
        return (rows == ids - step * CHUNK).astype(F32).astype(BF16)

    lane_rows = lax.broadcasted_iota(jnp.int32, (CHUNK, 128), 0)
    for step in range(PARTS // CHUNK):
        total = jnp.zeros((CHUNK, 128), F32)
        for k in range(neg.shape[1] // 128):
            total = total + (lane_rows == neg[:, k * 128:(k + 1) * 128] - step * CHUNK).astype(F32)
        counts[step * CHUNK:(step + 1) * CHUNK, :] = jnp.broadcast_to(
            jnp.sum(total, axis=1, keepdims=True) * weight, (CHUNK, 128)
        )

    w = jnp.zeros((D, EDGES), F32)
    h = jnp.zeros((D, EDGES), F32)
    t = jnp.zeros((D, EDGES), F32)
    for step in range(PARTS // CHUNK):
        table = table_ref[step * CHUNK:(step + 1) * CHUNK, :]
        high = table.astype(BF16)
        low = (table - high.astype(F32)).astype(BF16)
        hot = one_hot(rel, step)
        w = w + dot(high, hot, 0, 0) + dot(low, hot, 0, 0)
        h = h + dot(chunk_of(mine_ref, other_ref, 0, step), one_hot(lhs, step), 0, 0)
        t = t + dot(chunk_of(mine_ref, other_ref, 1, step), one_hot(rhs, step), 0, 0)
    w_re, w_im, h_re, h_im = w[:HALF], w[HALF:], h[:HALF], h[HALF:]
    query = jnp.concatenate([h_re * w_re - h_im * w_im, h_re * w_im + h_im * w_re], axis=0).astype(BF16)
    pos = jnp.sum(query.astype(F32) * t, axis=0, keepdims=True)
    pos_grad = (0.5 * jnp.tanh(0.5 * pos) - 0.5) * alive

    grad = jnp.zeros((D, EDGES), F32)
    for step in range(PARTS // CHUNK):
        tails = chunk_of(mine_ref, other_ref, 1, step)
        scores = dot(tails, query, 1, 0)
        often = counts[step * CHUNK:(step + 1) * CHUNK, :]
        often = jnp.concatenate([often] * (EDGES // 128), axis=1)
        both = (0.5 * jnp.tanh(0.5 * scores) + 0.5) * often * alive
        both = both + jnp.where(rows == rhs - step * CHUNK, pos_grad, 0.0)
        both = both.astype(BF16)
        grad = grad + dot(tails, both, 0, 0)
        out = dot(both, query, 1, 1).astype(BF16)
        ref = mine_out if step < 2 else other_out
        s = 2 * (step % 2)
        ref[s, SHARD:, :] = out[:SHARD]
        ref[s + 1, SHARD:, :] = out[SHARD:]

    g_re, g_im = grad[:HALF], grad[HALF:]
    head = jnp.concatenate([g_re * w_re + g_im * w_im, g_im * w_re - g_re * w_im], axis=0).astype(BF16)
    term = jnp.concatenate([g_re * h_re + g_im * h_im, g_im * h_re - g_re * h_im], axis=0).astype(BF16)
    for step in range(PARTS // CHUNK):
        out = dot(one_hot(lhs, step), head, 1, 1).astype(BF16)
        ref = mine_out if step < 2 else other_out
        s = 2 * (step % 2)
        ref[s, :SHARD, :] = out[:SHARD]
        ref[s + 1, :SHARD, :] = out[SHARD:]
        out = dot(one_hot(rel, step), term, 1, 1).astype(BF16)
        rel_out[2 * step] = out[:SHARD]
        rel_out[2 * step + 1] = out[SHARD:]


def edge_terms(scalars, lhs, rhs, rel, neg, mine, other, table):
    vmem = pl.BlockSpec(memory_space=pltpu.VMEM)
    block = jax.ShapeDtypeStruct((4, 2 * SHARD, D), BF16)
    return pl.pallas_call(
        edge_kernel,
        out_shape=(block, block, jax.ShapeDtypeStruct((8, SHARD, D), BF16)),
        in_specs=[pl.BlockSpec(memory_space=pltpu.SMEM)] + [vmem] * 7,
        out_specs=(vmem, vmem, vmem),
        scratch_shapes=[pltpu.VMEM((PARTS, 128), F32)],
        compiler_params=pltpu.CompilerParams(vmem_limit_bytes=40 << 20),
    )(scalars, lhs, rhs, rel, neg, mine, other, table)


def swap(block, axis, distance=1):
    size = lax.axis_size(axis)
    return lax.ppermute(block, axis, [(i, i ^ distance) for i in range(size)])


def spread(block, axis, size):
    copies = jnp.broadcast_to(block[None], (size,) + block.shape)
    return lax.all_to_all(copies, axis, 0, 0)


def summed(blocks, axis):
    return jnp.sum(lax.all_to_all(blocks, axis, 0, 0).astype(F32), axis=0)


def tie(*values):
    return lax.optimization_barrier(values)


def local(embeddings, relations, lhs_ids, rhs_ids, rel_ids, neg_ids, live):
    zh = lax.axis_index("zh")
    tails = swap(embeddings, "yh")
    mine = spread(jnp.concatenate([embeddings, tails], axis=0), "zh", 4)
    other = swap(mine, "core")
    scalars = jnp.concatenate([live, lax.axis_index("core").astype(jnp.int32)[None]])
    mine_sum, other_sum, rel_part = edge_terms(
        scalars, lhs_ids[0], rhs_ids[0], rel_ids[0], neg_ids[0, 0], mine, other, relations
    )
    from_core = swap(other_sum, "core")
    rel_xz = summed(rel_part, XZ).astype(BF16)
    from_core, rel_xz = tie(from_core, rel_xz)

    chip = (mine_sum.astype(F32) + from_core.astype(F32)).astype(BF16)
    high = zh // 2
    pairs = chip.reshape(2, 2, 2 * SHARD, D)
    keep = lax.dynamic_index_in_dim(pairs, high, 0, keepdims=False)
    from_two = swap(lax.dynamic_index_in_dim(pairs, 1 - high, 0, keepdims=False), "zh", 2)
    rel_y = summed(rel_xz.reshape(8, 16, D), Y).astype(BF16)
    from_two, rel_y = tie(from_two, rel_y)

    quad = (keep.astype(F32) + from_two.astype(F32)).astype(BF16)
    low = zh % 2
    keep = lax.dynamic_index_in_dim(quad, low, 0, keepdims=False)
    from_one = swap(lax.dynamic_index_in_dim(quad, 1 - low, 0, keepdims=False), "zh", 1)
    rel_all_y = spread(rel_y, Y, 8).reshape(SHARD, D)
    from_one, rel_all_y = tie(from_one, rel_all_y)

    shard = keep.astype(F32) + from_one.astype(F32)
    back = swap(shard[SHARD:].astype(BF16), "yh")
    rel_all = spread(rel_all_y, XZ, 8).reshape(PARTS, D)
    return shard[:SHARD] + back.astype(F32), rel_all.astype(F32)


def solution(mesh):
    fine = Mesh(mesh.devices.reshape(2, 4, 4, 2, 4, 2), AXES)
    dom, rel = AXES[:4], AXES[4:]
    placed = (
        P(AXES, None),
        P(rel, None),
        P(dom, rel, None),
        P(dom, rel, None),
        P(dom, rel, None),
        P(dom, rel, None, None),
        P(AXES),
    )
    return jax.shard_map(
        local,
        mesh=fine,
        in_specs=placed,
        out_specs=(P(AXES, None), P(rel, None)),
        check_vma=False,
    )
```

```python
import jax
import jax.numpy as jnp
from jax import lax
from jax.experimental import pallas as pl
from jax.experimental.pallas import tpu as pltpu
from jax.sharding import Mesh
from jax.sharding import PartitionSpec as P

F32 = jnp.float32
BF16 = jnp.bfloat16
AXES = ("yh", "yl", "x", "zl", "zh", "core")
Y = ("yh", "yl")
XZ = ("x", "zl")

D = 256
HALF = 128
SHARD = 128
EDGES = 512
CHUNK = 256
PARTS = 1024


def dot(a, b, ca, cb):
    return lax.dot_general(a, b, (((ca,), (cb,)), ((), ())), preferred_element_type=F32)


def place(ids, core):
    owner = jnp.bitwise_and(jnp.right_shift(ids, 7), 1)
    side = jnp.where(owner == core, 0, 512)
    return side + jnp.right_shift(ids, 8) * SHARD + jnp.bitwise_and(ids, SHARD - 1)


def one_hot(ids, step):
    rows = lax.broadcasted_iota(jnp.int32, (CHUNK, EDGES), 0)
    return (rows == ids - step * CHUNK).astype(F32).astype(BF16)


def early_kernel(scal_ref, rel_ref, neg_ref, table_ref, w_out, counts_out):
    weight = neg_ref.shape[1] ** (-0.5)
    neg = place(neg_ref[...], scal_ref[1])
    rel = rel_ref[...]
    lane_rows = lax.broadcasted_iota(jnp.int32, (CHUNK, 128), 0)
    w = jnp.zeros((D, EDGES), F32)
    for step in range(PARTS // CHUNK):
        table = table_ref[step * CHUNK:(step + 1) * CHUNK, :]
        high = table.astype(BF16)
        low = (table - high.astype(F32)).astype(BF16)
        hot = one_hot(rel, step)
        w = w + dot(high, hot, 0, 0) + dot(low, hot, 0, 0)
        total = jnp.zeros((CHUNK, 128), F32)
        for k in range(neg.shape[1] // 128):
            total = total + (lane_rows == neg[:, k * 128:(k + 1) * 128] - step * CHUNK).astype(F32)
        counts_out[step * CHUNK:(step + 1) * CHUNK, :] = jnp.broadcast_to(
            jnp.sum(total, axis=1, keepdims=True) * weight, (CHUNK, 128)
        )
    w_out[...] = w


def edge_kernel(
    scal_ref, lhs_ref, rhs_ref, rel_ref, w_ref, counts_ref, mine_ref, other_ref,
    mine_out, other_out, rel_out,
):
    live, core = scal_ref[0], scal_ref[1]

    def chunk_of(part, step):
        ref = mine_ref if step < 2 else other_ref
        s = 2 * (step % 2)
        rows = slice(part * SHARD, (part + 1) * SHARD)
        return jnp.concatenate([ref[s, rows], ref[s + 1, rows]], axis=0)

    def store(part, step, out):
        ref = mine_out if step < 2 else other_out
        s = 2 * (step % 2)
        rows = slice(part * SHARD, (part + 1) * SHARD)
        ref[s, rows, :] = out[:SHARD]
        ref[s + 1, rows, :] = out[SHARD:]

    lhs = place(lhs_ref[...], core)
    rhs = place(rhs_ref[...], core)
    rel = rel_ref[...]
    alive = (lax.broadcasted_iota(jnp.int32, (1, EDGES), 1) < live).astype(F32)
    rows = lax.broadcasted_iota(jnp.int32, (CHUNK, EDGES), 0)

    h = jnp.zeros((D, EDGES), F32)
    t = jnp.zeros((D, EDGES), F32)
    for step in range(PARTS // CHUNK):
        h = h + dot(chunk_of(0, step), one_hot(lhs, step), 0, 0)
        t = t + dot(chunk_of(1, step), one_hot(rhs, step), 0, 0)
    w_re, w_im, h_re, h_im = w_ref[:HALF], w_ref[HALF:], h[:HALF], h[HALF:]
    query = jnp.concatenate([h_re * w_re - h_im * w_im, h_re * w_im + h_im * w_re], axis=0).astype(BF16)
    pos = jnp.sum(query.astype(F32) * t, axis=0, keepdims=True)
    pos_grad = (0.5 * jnp.tanh(0.5 * pos) - 0.5) * alive

    grad = jnp.zeros((D, EDGES), F32)
    for step in range(PARTS // CHUNK):
        tails = chunk_of(1, step)
        scores = dot(tails, query, 1, 0)
        often = counts_ref[step * CHUNK:(step + 1) * CHUNK, :]
        often = jnp.concatenate([often] * (EDGES // 128), axis=1)
        both = (0.5 * jnp.tanh(0.5 * scores) + 0.5) * often * alive
        both = both + jnp.where(rows == rhs - step * CHUNK, pos_grad, 0.0)
        both = both.astype(BF16)
        grad = grad + dot(tails, both, 0, 0)
        store(1, step, dot(both, query, 1, 1).astype(BF16))

    g_re, g_im = grad[:HALF], grad[HALF:]
    term = jnp.concatenate([g_re * h_re + g_im * h_im, g_im * h_re - g_re * h_im], axis=0).astype(BF16)
    head = jnp.concatenate([g_re * w_re + g_im * w_im, g_im * w_re - g_re * w_im], axis=0).astype(BF16)
    for step in range(PARTS // CHUNK):
        out = dot(one_hot(rel, step), term, 1, 1).astype(BF16)
        rel_out[2 * step] = out[:SHARD]
        rel_out[2 * step + 1] = out[SHARD:]
        store(0, step, dot(one_hot(lhs, step), head, 1, 1).astype(BF16))


def early_terms(scalars, rel, neg, table):
    vmem = pl.BlockSpec(memory_space=pltpu.VMEM)
    return pl.pallas_call(
        early_kernel,
        out_shape=(jax.ShapeDtypeStruct((D, EDGES), F32), jax.ShapeDtypeStruct((PARTS, 128), F32)),
        in_specs=[pl.BlockSpec(memory_space=pltpu.SMEM)] + [vmem] * 3,
        out_specs=(vmem, vmem),
        compiler_params=pltpu.CompilerParams(vmem_limit_bytes=24 << 20),
        cost_estimate=pl.CostEstimate(flops=1 << 30, bytes_accessed=3 << 20, transcendentals=0),
    )(scalars, rel, neg, table)


def edge_terms(scalars, lhs, rhs, rel, w, counts, mine, other):
    vmem = pl.BlockSpec(memory_space=pltpu.VMEM)
    block = jax.ShapeDtypeStruct((4, 2 * SHARD, D), BF16)
    return pl.pallas_call(
        edge_kernel,
        out_shape=(block, block, jax.ShapeDtypeStruct((8, SHARD, D), BF16)),
        in_specs=[pl.BlockSpec(memory_space=pltpu.SMEM)] + [vmem] * 7,
        out_specs=(vmem, vmem, vmem),
        compiler_params=pltpu.CompilerParams(vmem_limit_bytes=40 << 20),
    )(scalars, lhs, rhs, rel, w, counts, mine, other)


def swap(block, axis, distance=1):
    size = lax.axis_size(axis)
    return lax.ppermute(block, axis, [(i, i ^ distance) for i in range(size)])


def spread(block, axis, size):
    copies = jnp.broadcast_to(block[None], (size,) + block.shape)
    return lax.all_to_all(copies, axis, 0, 0)


def summed(blocks):
    return jnp.sum(blocks.astype(F32), axis=0).astype(BF16)


def exchange(blocks, axis):
    return lax.all_to_all(blocks, axis, 0, 0)


def tie(*values):
    return lax.optimization_barrier(values)


def local(embeddings, relations, lhs_ids, rhs_ids, rel_ids, neg_ids, live):
    zh = lax.axis_index("zh")
    scalars = jnp.concatenate([live, lax.axis_index("core").astype(jnp.int32)[None]])
    tails = swap(embeddings, "yh")
    w, counts = early_terms(scalars, rel_ids[0], neg_ids[0, 0], relations)
    tails, w, counts = tie(tails, w, counts)
    both = jnp.concatenate([embeddings, tails], axis=0)
    mine = lax.all_gather(both, "zh", axis=0, tiled=False)
    other = swap(mine, "core")
    mine_sum, other_sum, rel_part = edge_terms(
        scalars, lhs_ids[0], rhs_ids[0], rel_ids[0], w, counts, mine, other
    )
    from_core = swap(other_sum, "core")
    parts = exchange(rel_part, XZ)
    from_core, parts = tie(from_core, parts)

    chip = (mine_sum.astype(F32) + from_core.astype(F32)).astype(BF16)
    keep = lax.dynamic_index_in_dim(chip, zh, 0, keepdims=False)
    arrived = []
    for step in (1, 3, 2):
        block = lax.dynamic_index_in_dim(chip, (zh + step) % 4, 0, keepdims=False)
        arrived.append(lax.ppermute(block, "zh", [(i, (i + step) % 4) for i in range(4)]))
    parts = spread(summed(parts), Y, 8)
    *arrived, parts = tie(*arrived, parts)

    shard = keep.astype(F32)
    for block in arrived:
        shard = shard + block.astype(F32)
    back = swap(shard[SHARD:].astype(BF16), "yh")
    rel_all = spread(summed(parts), XZ, 8).reshape(PARTS, D)
    return shard[:SHARD] + back.astype(F32), rel_all.astype(F32)


def solution(mesh):
    fine = Mesh(mesh.devices.reshape(2, 4, 4, 2, 4, 2), AXES)
    dom, rel = AXES[:4], AXES[4:]
    placed = (
        P(AXES, None),
        P(rel, None),
        P(dom, rel, None),
        P(dom, rel, None),
        P(dom, rel, None),
        P(dom, rel, None, None),
        P(AXES),
    )
    return jax.shard_map(
        local,
        mesh=fine,
        in_specs=placed,
        out_specs=(P(AXES, None), P(rel, None)),
        check_vma=False,
    )
```

```python
import jax
import jax.numpy as jnp
from jax import lax
from jax.experimental import pallas as pl
from jax.experimental.pallas import tpu as pltpu
from jax.sharding import Mesh
from jax.sharding import PartitionSpec as P

F32 = jnp.float32
BF16 = jnp.bfloat16
AXES = ("yh", "yl", "x", "zl", "zh", "core")
NEAR = ("x", "zl")
FAR = ("yh", "yl")

D = 256
HALF = 128
SHARD = 128
EDGES = 512
CHUNK = 256
PARTS = 1024


def dot(a, b, ca, cb):
    return lax.dot_general(a, b, (((ca,), (cb,)), ((), ())), preferred_element_type=F32)


LHS, RHS, REL, NEG, LIVE = 0, 2, 4, 6, 14
PACK_ROWS = 16
NEGATIVES = 2048


def pack_ids(lhs, rhs, rel, neg, live):
    rest = jnp.zeros((PACK_ROWS * 256 - 3 * EDGES - NEGATIVES - 1,), jnp.int32)
    ids = jnp.concatenate([lhs, rhs, rel, neg, live, rest]).reshape(PACK_ROWS, 256)
    return jnp.concatenate([jnp.right_shift(ids, 5), jnp.bitwise_and(ids, 31)], axis=0).astype(BF16)


def unpack(block, start, stop):
    wide = block[SHARD:].astype(F32)
    ids = wide[:PACK_ROWS] * 32.0 + wide[PACK_ROWS:]
    return jnp.concatenate([ids[k:k + 1] for k in range(start, stop)], axis=1).astype(jnp.int32)


def place(ids, core):
    owner = jnp.bitwise_and(jnp.right_shift(ids, 7), 1)
    side = jnp.where(owner == core, 0, 512)
    return side + jnp.right_shift(ids, 8) * SHARD + jnp.bitwise_and(ids, SHARD - 1)


def one_hot(ids, step):
    rows = lax.broadcasted_iota(jnp.int32, (CHUNK, EDGES), 0)
    return (rows == ids - step * CHUNK).astype(F32).astype(BF16)


def early_kernel(core_ref, block_ref, table_ref, w_out, counts_out):
    lane_rows = lax.broadcasted_iota(jnp.int32, (CHUNK, 128), 0)
    block = block_ref[...]
    rel = unpack(block, REL, NEG)
    neg = place(unpack(block, NEG, LIVE), core_ref[0])
    w = jnp.zeros((D, EDGES), F32)
    for step in range(PARTS // CHUNK):
        table = table_ref[step * CHUNK:(step + 1) * CHUNK, :]
        high = table.astype(BF16)
        low = (table - high.astype(F32)).astype(BF16)
        hot = one_hot(rel, step)
        w = w + dot(high, hot, 0, 0) + dot(low, hot, 0, 0)
        found = jnp.zeros((CHUNK, 128), F32)
        for k in range(NEGATIVES // 128):
            found = found + (lane_rows == neg[:, k * 128:(k + 1) * 128] - step * CHUNK).astype(F32)
        counts_out[step * CHUNK:(step + 1) * CHUNK, :] = jnp.broadcast_to(
            jnp.sum(found, axis=1, keepdims=True) * NEGATIVES ** (-0.5), (CHUNK, 128)
        )
    w_out[...] = w


def edge_kernel(
    core_ref, zh_ref, block_a, block_b, w_a, w_b, counts_a, counts_b, mine_ref, other_ref,
    mine_out, other_out, rel_out,
):
    core, zh = core_ref[0], zh_ref[0]
    pack_a, pack_b = block_a[...], block_b[...]
    rows = lax.broadcasted_iota(jnp.int32, (CHUNK, EDGES), 0)
    lanes = lax.broadcasted_iota(jnp.int32, (1, EDGES), 1)
    steps = range(PARTS // CHUNK)

    def chunk_of(part, step):
        ref = mine_ref if step < 2 else other_ref
        s = 2 * (step % 2)
        here = slice(part * SHARD, (part + 1) * SHARD)
        return jnp.concatenate([ref[s, here], ref[s + 1, here]], axis=0)

    def queries(pack, w_ref, head_part):
        lhs = place(unpack(pack, LHS, RHS), core)
        rhs = place(unpack(pack, RHS, REL), core)
        alive = (lanes < unpack(pack, LIVE, LIVE + 1)[:, :1]).astype(F32)
        h = jnp.zeros((D, EDGES), F32)
        t = jnp.zeros((D, EDGES), F32)
        for step in steps:
            h = h + dot(chunk_of(head_part, step), one_hot(lhs, step), 0, 0)
            t = t + dot(chunk_of(1 - head_part, step), one_hot(rhs, step), 0, 0)
        w_re, w_im, h_re, h_im = w_ref[:HALF], w_ref[HALF:], h[:HALF], h[HALF:]
        query = jnp.concatenate(
            [h_re * w_re - h_im * w_im, h_re * w_im + h_im * w_re], axis=0
        ).astype(BF16)
        pos = jnp.sum(query.astype(F32) * t, axis=0, keepdims=True)
        pos_grad = (0.5 * jnp.tanh(0.5 * pos) - 0.5) * alive
        return lhs, rhs, alive, h, query, pos_grad

    def score_grads(tails, query, counts_ref, step, rhs, alive, pos_grad):
        scores = dot(tails, query, 1, 0)
        often = counts_ref[step * CHUNK:(step + 1) * CHUNK, :]
        often = jnp.concatenate([often] * (EDGES // 128), axis=1)
        both = (0.5 * jnp.tanh(0.5 * scores) + 0.5) * often * alive
        return (both + jnp.where(rows == rhs - step * CHUNK, pos_grad, 0.0)).astype(BF16)

    lhs, rhs, alive, h, query, pos_grad = queries(pack_a, w_a, 0)
    grad = jnp.zeros((D, EDGES), F32)
    for step in steps:
        tails = chunk_of(1, step)
        both = score_grads(tails, query, counts_a, step, rhs, alive, pos_grad)
        grad = grad + dot(tails, both, 0, 0)
    g_re, g_im = grad[:HALF], grad[HALF:]
    h_re, h_im, w_re, w_im = h[:HALF], h[HALF:], w_a[:HALF], w_a[HALF:]
    term = jnp.concatenate([g_re * h_re + g_im * h_im, g_im * h_re - g_re * h_im], axis=0).astype(BF16)
    head = jnp.concatenate([g_re * w_re + g_im * w_im, g_im * w_re - g_re * w_im], axis=0).astype(BF16)

    _, rhs, alive, _, query, pos_grad = queries(pack_b, w_b, 1)
    rel = unpack(pack_a, REL, NEG)
    for step in steps:
        both = score_grads(chunk_of(0, step), query, counts_b, step, rhs, alive, pos_grad)
        out = (dot(both, query, 1, 1) + dot(one_hot(lhs, step), head, 1, 1)).astype(BF16)
        for half in range(2):
            d = jnp.bitwise_and(2 * (step % 2) + half - zh, 3)
            ref = mine_out if step < 2 else other_out
            ref[d] = out[half * SHARD:(half + 1) * SHARD]
        out = dot(one_hot(rel, step), term, 1, 1).astype(BF16)
        rel_out[2 * step] = out[:SHARD]
        rel_out[2 * step + 1] = out[SHARD:]


def early_terms(core, block, table):
    vmem = pl.BlockSpec(memory_space=pltpu.VMEM)
    return pl.pallas_call(
        early_kernel,
        out_shape=(jax.ShapeDtypeStruct((D, EDGES), F32), jax.ShapeDtypeStruct((PARTS, 128), F32)),
        in_specs=[pl.BlockSpec(memory_space=pltpu.SMEM)] + [vmem] * 2,
        out_specs=(vmem, vmem),
        compiler_params=pltpu.CompilerParams(vmem_limit_bytes=24 << 20),
        cost_estimate=pl.CostEstimate(flops=1 << 30, bytes_accessed=3 << 20, transcendentals=0),
    )(core, block, table)


def edge_terms(core, zh, block_a, block_b, w_a, w_b, counts_a, counts_b, mine, other):
    vmem = pl.BlockSpec(memory_space=pltpu.VMEM)
    block = jax.ShapeDtypeStruct((4, SHARD, D), BF16)
    return pl.pallas_call(
        edge_kernel,
        out_shape=(block, block, jax.ShapeDtypeStruct((8, SHARD, D), BF16)),
        in_specs=[pl.BlockSpec(memory_space=pltpu.SMEM)] * 2 + [vmem] * 8,
        out_specs=(vmem, vmem, vmem),
        compiler_params=pltpu.CompilerParams(vmem_limit_bytes=40 << 20),
    )(core, zh, block_a, block_b, w_a, w_b, counts_a, counts_b, mine, other)


def swap(block, axis, distance=1):
    size = lax.axis_size(axis)
    return lax.ppermute(block, axis, [(i, i ^ distance) for i in range(size)])


def spread(block, axis, size):
    copies = jnp.broadcast_to(block[None], (size,) + block.shape)
    return lax.all_to_all(copies, axis, 0, 0)


def summed(blocks):
    return jnp.sum(blocks.astype(F32), axis=0).astype(BF16)


def exchange(blocks, axis):
    return lax.all_to_all(blocks, axis, 0, 0)


def tie(*values):
    return lax.optimization_barrier(values)


def local(embeddings, relations, lhs_ids, rhs_ids, rel_ids, neg_ids, live):
    core = lax.axis_index("core").astype(jnp.int32)[None]
    zh = lax.axis_index("zh").astype(jnp.int32)[None]
    ids = pack_ids(lhs_ids[0, 0], rhs_ids[0, 0], rel_ids[0, 0], neg_ids[0, 0, 0], live)
    block_a = jnp.concatenate([embeddings, ids], axis=0)
    block_b = swap(block_a, "yh")
    w_a, counts_a = early_terms(core, block_a, relations)
    block_b, w_a, counts_a = tie(block_b, w_a, counts_a)
    both = jnp.concatenate([embeddings, block_b[:SHARD]], axis=0)
    mine = lax.all_gather(both, "zh", axis=0, tiled=False)
    other = swap(mine, "core")
    w_b, counts_b = early_terms(core, block_b, relations)
    mine_sum, other_sum, rel_part = edge_terms(
        core, zh, block_a, block_b, w_a, w_b, counts_a, counts_b, mine, other
    )
    from_core = swap(other_sum, "core")
    parts = exchange(rel_part, NEAR)
    from_core, parts = tie(from_core, parts)
    chip = (mine_sum.astype(F32) + from_core.astype(F32)).astype(BF16)
    arrived = [
        lax.ppermute(chip[step], "zh", [(i, (i + step) % 4) for i in range(4)]) for step in (1, 3, 2)
    ]
    parts = spread(summed(parts), FAR, 8)
    *arrived, parts = tie(*arrived, parts)
    shard = chip[0].astype(F32)
    for block in arrived:
        shard = shard + block.astype(F32)
    rel_all = spread(summed(parts), NEAR, 8).reshape(PARTS, D)
    return shard, rel_all.astype(F32)


def solution(mesh):
    fine = Mesh(mesh.devices.reshape(2, 4, 4, 2, 4, 2), AXES)
    dom, rel = AXES[:4], AXES[4:]
    placed = (
        P(AXES, None),
        P(rel, None),
        P(dom, rel, None),
        P(dom, rel, None),
        P(dom, rel, None),
        P(dom, rel, None, None),
        P(AXES),
    )
    return jax.shard_map(
        local,
        mesh=fine,
        in_specs=placed,
        out_specs=(P(AXES, None), P(rel, None)),
        check_vma=False,
    )
```

```python
import jax
import jax.numpy as jnp
from jax import lax
from jax.experimental import pallas as pl
from jax.experimental.pallas import tpu as pltpu
from jax.sharding import Mesh
from jax.sharding import PartitionSpec as P

F32 = jnp.float32
BF16 = jnp.bfloat16
AXES = ("yh", "ym", "yl", "x", "zl", "zh", "core")
NEAR = ("yl", "x", "zl")
FAR = ("yh", "ym")

D = 256
HALF = 128
SHARD = 128
EDGES = 512
CHUNK = 256
PARTS = 1024


def dot(a, b, ca, cb):
    return lax.dot_general(a, b, (((ca,), (cb,)), ((), ())), preferred_element_type=F32)


LHS, RHS, REL, NEG, LIVE = 0, 2, 4, 6, 14
PACK_ROWS = 16
NEGATIVES = 2048


def pack_ids(lhs, rhs, rel, neg, live):
    rest = jnp.zeros((PACK_ROWS * 256 - 3 * EDGES - NEGATIVES - 1,), jnp.int32)
    ids = jnp.concatenate([lhs, rhs, rel, neg, live, rest]).reshape(PACK_ROWS, 256)
    return jnp.concatenate([jnp.right_shift(ids, 5), jnp.bitwise_and(ids, 31)], axis=0).astype(BF16)


def unpack(block, start, stop):
    wide = block[SHARD:].astype(F32)
    ids = wide[:PACK_ROWS] * 32.0 + wide[PACK_ROWS:]
    return jnp.concatenate([ids[k:k + 1] for k in range(start, stop)], axis=1).astype(jnp.int32)


def place(ids, core):
    owner = jnp.bitwise_and(jnp.right_shift(ids, 7), 1)
    side = jnp.where(owner == core, 0, 512)
    return side + jnp.right_shift(ids, 8) * SHARD + jnp.bitwise_and(ids, SHARD - 1)


def one_hot(ids, step):
    rows = lax.broadcasted_iota(jnp.int32, (CHUNK, EDGES), 0)
    return (rows == ids - step * CHUNK).astype(F32).astype(BF16)


def early_kernel(core_ref, block_ref, table_ref, w_out, counts_out):
    lane_rows = lax.broadcasted_iota(jnp.int32, (CHUNK, 128), 0)
    block = block_ref[...]
    rel = unpack(block, REL, NEG)
    neg = place(unpack(block, NEG, LIVE), core_ref[0])
    w = jnp.zeros((D, EDGES), F32)
    for step in range(PARTS // CHUNK):
        table = table_ref[step * CHUNK:(step + 1) * CHUNK, :]
        high = table.astype(BF16)
        low = (table - high.astype(F32)).astype(BF16)
        hot = one_hot(rel, step)
        w = w + dot(high, hot, 0, 0) + dot(low, hot, 0, 0)
        found = jnp.zeros((CHUNK, 128), F32)
        for k in range(NEGATIVES // 128):
            found = found + (lane_rows == neg[:, k * 128:(k + 1) * 128] - step * CHUNK).astype(F32)
        counts_out[step * CHUNK:(step + 1) * CHUNK, :] = jnp.broadcast_to(
            jnp.sum(found, axis=1, keepdims=True) * NEGATIVES ** (-0.5), (CHUNK, 128)
        )
    w_out[...] = w


def edge_kernel(
    core_ref, zh_ref, block_a, block_b, w_a, w_b, counts_a, counts_b, mine_ref, other_ref,
    mine_out, other_out, rel_out,
):
    core, zh = core_ref[0], zh_ref[0]
    pack_a, pack_b = block_a[...], block_b[...]
    rows = lax.broadcasted_iota(jnp.int32, (CHUNK, EDGES), 0)
    lanes = lax.broadcasted_iota(jnp.int32, (1, EDGES), 1)
    steps = range(PARTS // CHUNK)

    def chunk_of(part, step):
        ref = mine_ref if step < 2 else other_ref
        s = 2 * (step % 2)
        here = slice(part * SHARD, (part + 1) * SHARD)
        return jnp.concatenate([ref[s, here], ref[s + 1, here]], axis=0)

    def queries(pack, w_ref, head_part):
        lhs = place(unpack(pack, LHS, RHS), core)
        rhs = place(unpack(pack, RHS, REL), core)
        alive = (lanes < unpack(pack, LIVE, LIVE + 1)[:, :1]).astype(F32)
        h = jnp.zeros((D, EDGES), F32)
        t = jnp.zeros((D, EDGES), F32)
        for step in steps:
            h = h + dot(chunk_of(head_part, step), one_hot(lhs, step), 0, 0)
            t = t + dot(chunk_of(1 - head_part, step), one_hot(rhs, step), 0, 0)
        w_re, w_im, h_re, h_im = w_ref[:HALF], w_ref[HALF:], h[:HALF], h[HALF:]
        query = jnp.concatenate(
            [h_re * w_re - h_im * w_im, h_re * w_im + h_im * w_re], axis=0
        ).astype(BF16)
        pos = jnp.sum(query.astype(F32) * t, axis=0, keepdims=True)
        pos_grad = (0.5 * jnp.tanh(0.5 * pos) - 0.5) * alive
        return lhs, rhs, alive, h, query, pos_grad

    def score_grads(tails, query, counts_ref, step, rhs, alive, pos_grad):
        scores = dot(tails, query, 1, 0)
        often = counts_ref[step * CHUNK:(step + 1) * CHUNK, :]
        often = jnp.concatenate([often] * (EDGES // 128), axis=1)
        both = (0.5 * jnp.tanh(0.5 * scores) + 0.5) * often * alive
        return (both + jnp.where(rows == rhs - step * CHUNK, pos_grad, 0.0)).astype(BF16)

    lhs, rhs, alive, h, query, pos_grad = queries(pack_a, w_a, 0)
    grad = jnp.zeros((D, EDGES), F32)
    for step in steps:
        tails = chunk_of(1, step)
        both = score_grads(tails, query, counts_a, step, rhs, alive, pos_grad)
        grad = grad + dot(tails, both, 0, 0)
    g_re, g_im = grad[:HALF], grad[HALF:]
    h_re, h_im, w_re, w_im = h[:HALF], h[HALF:], w_a[:HALF], w_a[HALF:]
    term = jnp.concatenate([g_re * h_re + g_im * h_im, g_im * h_re - g_re * h_im], axis=0).astype(BF16)
    head = jnp.concatenate([g_re * w_re + g_im * w_im, g_im * w_re - g_re * w_im], axis=0).astype(BF16)

    _, rhs, alive, _, query, pos_grad = queries(pack_b, w_b, 1)
    rel = unpack(pack_a, REL, NEG)
    for step in steps:
        both = score_grads(chunk_of(0, step), query, counts_b, step, rhs, alive, pos_grad)
        out = (dot(both, query, 1, 1) + dot(one_hot(lhs, step), head, 1, 1)).astype(BF16)
        for half in range(2):
            d = jnp.bitwise_and(2 * (step % 2) + half - zh, 3)
            ref = mine_out if step < 2 else other_out
            ref[d] = out[half * SHARD:(half + 1) * SHARD]
        out = dot(one_hot(rel, step), term, 1, 1).astype(BF16)
        for quarter in range(4):
            rel_out[4 * step + quarter] = out[quarter * 64:(quarter + 1) * 64]


def early_terms(core, block, table):
    vmem = pl.BlockSpec(memory_space=pltpu.VMEM)
    return pl.pallas_call(
        early_kernel,
        out_shape=(jax.ShapeDtypeStruct((D, EDGES), F32), jax.ShapeDtypeStruct((PARTS, 128), F32)),
        in_specs=[pl.BlockSpec(memory_space=pltpu.SMEM)] + [vmem] * 2,
        out_specs=(vmem, vmem),
        compiler_params=pltpu.CompilerParams(vmem_limit_bytes=24 << 20),
        cost_estimate=pl.CostEstimate(flops=1 << 30, bytes_accessed=3 << 20, transcendentals=0),
    )(core, block, table)


def edge_terms(core, zh, block_a, block_b, w_a, w_b, counts_a, counts_b, mine, other):
    vmem = pl.BlockSpec(memory_space=pltpu.VMEM)
    block = jax.ShapeDtypeStruct((4, SHARD, D), BF16)
    return pl.pallas_call(
        edge_kernel,
        out_shape=(block, block, jax.ShapeDtypeStruct((16, 64, D), BF16)),
        in_specs=[pl.BlockSpec(memory_space=pltpu.SMEM)] * 2 + [vmem] * 8,
        out_specs=(vmem, vmem, vmem),
        compiler_params=pltpu.CompilerParams(vmem_limit_bytes=40 << 20),
    )(core, zh, block_a, block_b, w_a, w_b, counts_a, counts_b, mine, other)


def swap(block, axis, distance=1):
    size = lax.axis_size(axis)
    return lax.ppermute(block, axis, [(i, i ^ distance) for i in range(size)])


def move(block, step):
    return lax.ppermute(block, "zh", [(i, (i + step) % 4) for i in range(4)])


def spread(block, axis, size):
    copies = jnp.broadcast_to(block[None], (size,) + block.shape)
    return lax.all_to_all(copies, axis, 0, 0)


def summed(blocks):
    return jnp.sum(blocks.astype(F32), axis=0).astype(BF16)


def exchange(blocks, axis):
    return lax.all_to_all(blocks, axis, 0, 0)


def tie(*values):
    return lax.optimization_barrier(values)


def local(embeddings, relations, lhs_ids, rhs_ids, rel_ids, neg_ids, live):
    core = lax.axis_index("core").astype(jnp.int32)[None]
    zh = lax.axis_index("zh").astype(jnp.int32)[None]
    ids = pack_ids(lhs_ids[0, 0], rhs_ids[0, 0], rel_ids[0, 0], neg_ids[0, 0, 0], live)
    block_a = jnp.concatenate([embeddings, ids], axis=0)
    block_b = swap(block_a, "yh")
    w_a, counts_a = early_terms(core, block_a, relations)
    block_b, w_a, counts_a = tie(block_b, w_a, counts_a)
    both = jnp.concatenate([embeddings, block_b[:SHARD]], axis=0)
    mine = lax.all_gather(both, "zh", axis=0, tiled=False)
    other = swap(mine, "core")
    w_b, counts_b = early_terms(core, block_b, relations)
    mine_sum, other_sum, rel_part = edge_terms(
        core, zh, block_a, block_b, w_a, w_b, counts_a, counts_b, mine, other
    )
    from_core = swap(other_sum, "core")
    parts = exchange(rel_part, NEAR)
    chip = mine_sum.astype(F32) + from_core.astype(F32)
    two = move(chip[2], 2)
    one, three = move(chip[1].astype(BF16), 1), move(chip[3].astype(BF16), 3)
    parts = spread(summed(parts), FAR, 4)
    two, one, parts = tie(two, one, parts)
    shard = chip[0] + two + one.astype(F32) + three.astype(F32)
    rel_all = spread(summed(parts), NEAR, 16).reshape(PARTS, D)
    return shard, rel_all.astype(F32)


def solution(mesh):
    fine = Mesh(mesh.devices.reshape(2, 2, 2, 4, 2, 4, 2), AXES)
    dom, rel = AXES[:5], AXES[5:]
    placed = (
        P(AXES, None),
        P(rel, None),
        P(dom, rel, None),
        P(dom, rel, None),
        P(dom, rel, None),
        P(dom, rel, None, None),
        P(AXES),
    )
    return jax.shard_map(
        local,
        mesh=fine,
        in_specs=placed,
        out_specs=(P(AXES, None), P(rel, None)),
        check_vma=False,
    )
```

```python
import jax
import jax.numpy as jnp
from jax import lax
from jax.experimental import pallas as pl
from jax.experimental.pallas import tpu as pltpu
from jax.sharding import Mesh
from jax.sharding import PartitionSpec as P

F32 = jnp.float32
BF16 = jnp.bfloat16
AXES = ("yh", "ym", "yl", "x", "zl", "zh", "core")
NEAR = ("yl", "x", "zl")
FAR = ("yh", "ym")

D = 256
HALF = 128
SHARD = 128
EDGES = 512
CHUNK = 256
PARTS = 1024


def dot(a, b, ca, cb):
    return lax.dot_general(a, b, (((ca,), (cb,)), ((), ())), preferred_element_type=F32)


LHS, RHS, REL, NEG, LIVE = 0, 2, 4, 6, 14
PACK_ROWS = 16
NEGATIVES = 2048


def pack_ids(lhs, rhs, rel, neg, live):
    rest = jnp.zeros((PACK_ROWS * 256 - 3 * EDGES - NEGATIVES - 1,), jnp.int32)
    ids = jnp.concatenate([lhs, rhs, rel, neg, live, rest]).reshape(PACK_ROWS, 256)
    return jnp.concatenate([jnp.right_shift(ids, 5), jnp.bitwise_and(ids, 31)], axis=0).astype(BF16)


def unpack(block, start, stop):
    wide = block[SHARD:].astype(F32)
    ids = wide[:PACK_ROWS] * 32.0 + wide[PACK_ROWS:]
    return jnp.concatenate([ids[k:k + 1] for k in range(start, stop)], axis=1).astype(jnp.int32)


def place(ids, core):
    owner = jnp.bitwise_and(jnp.right_shift(ids, 7), 1)
    side = jnp.where(owner == core, 0, 512)
    return side + jnp.right_shift(ids, 8) * SHARD + jnp.bitwise_and(ids, SHARD - 1)


def one_hot(ids, step):
    rows = lax.broadcasted_iota(jnp.int32, (CHUNK, EDGES), 0)
    return (rows == ids - step * CHUNK).astype(F32).astype(BF16)


def early_kernel(core_ref, block_ref, table_ref, w_out, counts_out):
    lane_rows = lax.broadcasted_iota(jnp.int32, (CHUNK, 128), 0)
    block = block_ref[...]
    rel = unpack(block, REL, NEG)
    neg = place(unpack(block, NEG, LIVE), core_ref[0])
    w = jnp.zeros((D, EDGES), F32)
    for step in range(PARTS // CHUNK):
        table = table_ref[step * CHUNK:(step + 1) * CHUNK, :]
        high = table.astype(BF16)
        low = (table - high.astype(F32)).astype(BF16)
        hot = one_hot(rel, step)
        w = w + dot(high, hot, 0, 0) + dot(low, hot, 0, 0)
        found = jnp.zeros((CHUNK, 128), F32)
        for k in range(NEGATIVES // 128):
            found = found + (lane_rows == neg[:, k * 128:(k + 1) * 128] - step * CHUNK).astype(F32)
        counts_out[step * CHUNK:(step + 1) * CHUNK, :] = jnp.broadcast_to(
            jnp.sum(found, axis=1, keepdims=True) * NEGATIVES ** (-0.5), (CHUNK, 128)
        )
    w_out[...] = w


def edge_kernel(
    core_ref, zh_ref, block_a, block_b, w_a, w_b, counts_a, counts_b, mine_ref, other_ref,
    mine_out, other_out, rel_out,
):
    core, zh = core_ref[0], zh_ref[0]
    pack_a, pack_b = block_a[...], block_b[...]
    rows = lax.broadcasted_iota(jnp.int32, (CHUNK, EDGES), 0)
    lanes = lax.broadcasted_iota(jnp.int32, (1, EDGES), 1)
    steps = range(PARTS // CHUNK)

    def chunk_of(part, step):
        ref = mine_ref if step < 2 else other_ref
        s = 2 * (step % 2)
        here = slice(part * SHARD, (part + 1) * SHARD)
        return jnp.concatenate([ref[s, here], ref[s + 1, here]], axis=0)

    def queries(pack, w_ref, head_part):
        lhs = place(unpack(pack, LHS, RHS), core)
        rhs = place(unpack(pack, RHS, REL), core)
        alive = (lanes < unpack(pack, LIVE, LIVE + 1)[:, :1]).astype(F32)
        h = jnp.zeros((D, EDGES), F32)
        t = jnp.zeros((D, EDGES), F32)
        for step in steps:
            h = h + dot(chunk_of(head_part, step), one_hot(lhs, step), 0, 0)
            t = t + dot(chunk_of(1 - head_part, step), one_hot(rhs, step), 0, 0)
        w_re, w_im, h_re, h_im = w_ref[:HALF], w_ref[HALF:], h[:HALF], h[HALF:]
        query = jnp.concatenate(
            [h_re * w_re - h_im * w_im, h_re * w_im + h_im * w_re], axis=0
        ).astype(BF16)
        pos = jnp.sum(query.astype(F32) * t, axis=0, keepdims=True)
        pos_grad = (0.5 * jnp.tanh(0.5 * pos) - 0.5) * alive
        return lhs, rhs, alive, h, query, pos_grad

    def score_grads(tails, query, counts_ref, step, rhs, alive, pos_grad):
        scores = dot(tails, query, 1, 0)
        often = counts_ref[step * CHUNK:(step + 1) * CHUNK, :]
        often = jnp.concatenate([often] * (EDGES // 128), axis=1)
        both = (jnp.tanh(0.5 * scores) + 1.0) * (often * (0.5 * alive))
        return jnp.where(rows == rhs - step * CHUNK, both + pos_grad, both).astype(BF16)

    lhs, rhs, alive, h, query, pos_grad = queries(pack_a, w_a, 0)
    grad = jnp.zeros((D, EDGES), F32)
    for step in steps:
        tails = chunk_of(1, step)
        both = score_grads(tails, query, counts_a, step, rhs, alive, pos_grad)
        grad = grad + dot(tails, both, 0, 0)
    g_re, g_im = grad[:HALF], grad[HALF:]
    h_re, h_im, w_re, w_im = h[:HALF], h[HALF:], w_a[:HALF], w_a[HALF:]
    term = jnp.concatenate([g_re * h_re + g_im * h_im, g_im * h_re - g_re * h_im], axis=0).astype(BF16)
    head = jnp.concatenate([g_re * w_re + g_im * w_im, g_im * w_re - g_re * w_im], axis=0).astype(BF16)

    _, rhs, alive, _, query, pos_grad = queries(pack_b, w_b, 1)
    rel = unpack(pack_a, REL, NEG)
    for step in steps:
        both = score_grads(chunk_of(0, step), query, counts_b, step, rhs, alive, pos_grad)
        out = (dot(both, query, 1, 1) + dot(one_hot(lhs, step), head, 1, 1)).astype(BF16)
        for half in range(2):
            d = jnp.bitwise_xor(2 * (step % 2) + half, zh)
            ref = mine_out if step < 2 else other_out
            ref[d] = out[half * SHARD:(half + 1) * SHARD]
        out = dot(one_hot(rel, step), term, 1, 1).astype(BF16)
        for quarter in range(4):
            rel_out[4 * step + quarter] = out[quarter * 64:(quarter + 1) * 64]


def early_terms(core, block, table):
    vmem = pl.BlockSpec(memory_space=pltpu.VMEM)
    return pl.pallas_call(
        early_kernel,
        out_shape=(jax.ShapeDtypeStruct((D, EDGES), F32), jax.ShapeDtypeStruct((PARTS, 128), F32)),
        in_specs=[pl.BlockSpec(memory_space=pltpu.SMEM)] + [vmem] * 2,
        out_specs=(vmem, vmem),
        compiler_params=pltpu.CompilerParams(vmem_limit_bytes=24 << 20),
        cost_estimate=pl.CostEstimate(flops=1 << 30, bytes_accessed=3 << 20, transcendentals=0),
    )(core, block, table)


def edge_terms(core, zh, block_a, block_b, w_a, w_b, counts_a, counts_b, mine, other):
    vmem = pl.BlockSpec(memory_space=pltpu.VMEM)
    block = jax.ShapeDtypeStruct((4, SHARD, D), BF16)
    return pl.pallas_call(
        edge_kernel,
        out_shape=(block, block, jax.ShapeDtypeStruct((16, 64, D), BF16)),
        in_specs=[pl.BlockSpec(memory_space=pltpu.SMEM)] * 2 + [vmem] * 8,
        out_specs=(vmem, vmem, vmem),
        compiler_params=pltpu.CompilerParams(vmem_limit_bytes=40 << 20),
    )(core, zh, block_a, block_b, w_a, w_b, counts_a, counts_b, mine, other)


def swap(block, axis, distance=1):
    size = lax.axis_size(axis)
    return lax.ppermute(block, axis, [(i, i ^ distance) for i in range(size)])


def spread(block, axis, size):
    copies = jnp.broadcast_to(block[None], (size,) + block.shape)
    return lax.all_to_all(copies, axis, 0, 0)


def summed(blocks):
    return jnp.sum(blocks.astype(F32), axis=0).astype(BF16)


def exchange(blocks, axis):
    return lax.all_to_all(blocks, axis, 0, 0)


def tie(*values):
    return lax.optimization_barrier(values)


def local(embeddings, relations, lhs_ids, rhs_ids, rel_ids, neg_ids, live):
    core = lax.axis_index("core").astype(jnp.int32)[None]
    zh = lax.axis_index("zh").astype(jnp.int32)[None]
    ids = pack_ids(lhs_ids[0, 0], rhs_ids[0, 0], rel_ids[0, 0], neg_ids[0, 0, 0], live)
    block_a = jnp.concatenate([embeddings, ids], axis=0)
    block_b = swap(block_a, "yh")
    w_a, counts_a = early_terms(core, block_a, relations)
    block_b, w_a, counts_a = tie(block_b, w_a, counts_a)
    both = jnp.concatenate([embeddings, block_b[:SHARD]], axis=0)
    mine = lax.all_gather(both, "zh", axis=0, tiled=False)
    other = swap(mine, "core")
    w_b, counts_b = early_terms(core, block_b, relations)
    mine_sum, other_sum, rel_part = edge_terms(
        core, zh, block_a, block_b, w_a, w_b, counts_a, counts_b, mine, other
    )
    from_core = swap(other_sum, "core")
    parts = exchange(rel_part, NEAR)
    chip = mine_sum.astype(F32) + from_core.astype(F32)
    far = swap(chip[2:], "zh", 2)
    parts = spread(summed(parts), FAR, 4)
    far, parts = tie(far, parts)
    pair = chip[:2] + far
    near = swap(pair[1].astype(BF16), "zh", 1)
    shard = pair[0] + near.astype(F32)
    rel_all = spread(summed(parts), NEAR, 16).reshape(PARTS, D)
    return shard, rel_all.astype(F32)


def solution(mesh):
    fine = Mesh(mesh.devices.reshape(2, 2, 2, 4, 2, 4, 2), AXES)
    dom, rel = AXES[:5], AXES[5:]
    placed = (
        P(AXES, None),
        P(rel, None),
        P(dom, rel, None),
        P(dom, rel, None),
        P(dom, rel, None),
        P(dom, rel, None, None),
        P(AXES),
    )
    return jax.shard_map(
        local,
        mesh=fine,
        in_specs=placed,
        out_specs=(P(AXES, None), P(rel, None)),
        check_vma=False,
    )
```

```python
import jax
import jax.numpy as jnp
from jax import lax
from jax.experimental import pallas as pl
from jax.experimental.pallas import tpu as pltpu
from jax.sharding import Mesh
from jax.sharding import PartitionSpec as P

F32 = jnp.float32
BF16 = jnp.bfloat16
AXES = ("yh", "ym", "yl", "x", "zl", "zh", "core")
NEAR = ("yl", "x", "zl")
FAR = ("yh", "ym")

D = 256
HALF = 128
SHARD = 128
EDGES = 512
CHUNK = 256
PARTS = 1024


def dot(a, b, ca, cb):
    return lax.dot_general(a, b, (((ca,), (cb,)), ((), ())), preferred_element_type=F32)


LHS, RHS, REL, NEG, LIVE = 0, 2, 4, 6, 14
PACK_ROWS = 16
NEGATIVES = 2048


def pack_ids(lhs, rhs, rel, neg, live):
    rest = jnp.zeros((PACK_ROWS * 256 - 3 * EDGES - NEGATIVES - 1,), jnp.int32)
    ids = jnp.concatenate([lhs, rhs, rel, neg, live, rest]).reshape(PACK_ROWS, 256)
    return jnp.concatenate([jnp.right_shift(ids, 5), jnp.bitwise_and(ids, 31)], axis=0).astype(BF16)


def unpack(block, start, stop):
    wide = block[SHARD:].astype(F32)
    ids = wide[:PACK_ROWS] * 32.0 + wide[PACK_ROWS:]
    return jnp.concatenate([ids[k:k + 1] for k in range(start, stop)], axis=1).astype(jnp.int32)


def place(ids, core):
    owner = jnp.bitwise_and(jnp.right_shift(ids, 7), 1)
    side = jnp.where(owner == core, 0, 512)
    return side + jnp.right_shift(ids, 8) * SHARD + jnp.bitwise_and(ids, SHARD - 1)


def one_hot(ids, step):
    rows = lax.broadcasted_iota(jnp.int32, (CHUNK, EDGES), 0)
    return (rows == ids - step * CHUNK).astype(F32).astype(BF16)


def early_kernel(core_ref, block_ref, table_ref, w_out, counts_out):
    lane_rows = lax.broadcasted_iota(jnp.int32, (CHUNK, 128), 0)
    block = block_ref[...]
    rel = unpack(block, REL, NEG)
    neg = place(unpack(block, NEG, LIVE), core_ref[0])
    w = jnp.zeros((D, EDGES), F32)
    for step in range(PARTS // CHUNK):
        table = table_ref[step * CHUNK:(step + 1) * CHUNK, :]
        high = table.astype(BF16)
        low = (table - high.astype(F32)).astype(BF16)
        hot = one_hot(rel, step)
        w = w + dot(high, hot, 0, 0) + dot(low, hot, 0, 0)
        found = jnp.zeros((CHUNK, 128), F32)
        for k in range(NEGATIVES // 128):
            found = found + (lane_rows == neg[:, k * 128:(k + 1) * 128] - step * CHUNK).astype(F32)
        counts_out[step * CHUNK:(step + 1) * CHUNK, :] = jnp.broadcast_to(
            jnp.sum(found, axis=1, keepdims=True) * NEGATIVES ** (-0.5), (CHUNK, 128)
        )
    w_out[...] = w


def edge_kernel(
    core_ref, zh_ref, block_a, block_b, w_a, w_b, counts_a, counts_b, mine_ref, other_ref,
    mine_out, other_out, rel_out,
):
    core, zh = core_ref[0], zh_ref[0]
    pack_a, pack_b = block_a[...], block_b[...]
    rows = lax.broadcasted_iota(jnp.int32, (CHUNK, EDGES), 0)
    lanes = lax.broadcasted_iota(jnp.int32, (1, EDGES), 1)
    steps = range(PARTS // CHUNK)

    def chunk_of(part, step):
        ref = mine_ref if step < 2 else other_ref
        s = 2 * (step % 2)
        here = slice(part * SHARD, (part + 1) * SHARD)
        return jnp.concatenate([ref[s, here], ref[s + 1, here]], axis=0)

    def queries(pack, w_ref, head_part):
        lhs = place(unpack(pack, LHS, RHS), core)
        rhs = place(unpack(pack, RHS, REL), core)
        alive = (lanes < unpack(pack, LIVE, LIVE + 1)[:, :1]).astype(F32)
        h = jnp.zeros((D, EDGES), F32)
        t = jnp.zeros((D, EDGES), F32)
        for step in steps:
            h = h + dot(chunk_of(head_part, step), one_hot(lhs, step), 0, 0)
            t = t + dot(chunk_of(1 - head_part, step), one_hot(rhs, step), 0, 0)
        w_re, w_im, h_re, h_im = w_ref[:HALF], w_ref[HALF:], h[:HALF], h[HALF:]
        query = jnp.concatenate(
            [h_re * w_re - h_im * w_im, h_re * w_im + h_im * w_re], axis=0
        ).astype(BF16)
        pos = jnp.sum(query.astype(F32) * t, axis=0, keepdims=True)
        pos_grad = (0.5 * jnp.tanh(0.5 * pos) - 0.5) * alive
        return lhs, rhs, alive, h, query, pos_grad

    def score_grads(tails, query, counts_ref, step, rhs, alive, pos_grad):
        scores = dot(tails, query, 1, 0)
        often = counts_ref[step * CHUNK:(step + 1) * CHUNK, :]
        often = jnp.concatenate([often] * (EDGES // 128), axis=1)
        both = (jnp.tanh(0.5 * scores) + 1.0) * (often * (0.5 * alive))
        return jnp.where(rows == rhs - step * CHUNK, both + pos_grad, both).astype(BF16)

    lhs, rhs, alive, h, query, pos_grad = queries(pack_a, w_a, 0)
    grad = jnp.zeros((D, EDGES), F32)
    for step in steps:
        tails = chunk_of(1, step)
        both = score_grads(tails, query, counts_a, step, rhs, alive, pos_grad)
        grad = grad + dot(tails, both, 0, 0)
    g_re, g_im = grad[:HALF], grad[HALF:]
    h_re, h_im, w_re, w_im = h[:HALF], h[HALF:], w_a[:HALF], w_a[HALF:]
    term = jnp.concatenate([g_re * h_re + g_im * h_im, g_im * h_re - g_re * h_im], axis=0).astype(BF16)
    head = jnp.concatenate([g_re * w_re + g_im * w_im, g_im * w_re - g_re * w_im], axis=0).astype(BF16)

    _, rhs, alive, _, query, pos_grad = queries(pack_b, w_b, 1)
    rel = unpack(pack_a, REL, NEG)
    for step in steps:
        both = score_grads(chunk_of(0, step), query, counts_b, step, rhs, alive, pos_grad)
        out = (dot(both, query, 1, 1) + dot(one_hot(lhs, step), head, 1, 1)).astype(BF16)
        for half in range(2):
            d = jnp.bitwise_xor(2 * (step % 2) + half, zh)
            ref = mine_out if step < 2 else other_out
            ref[d] = out[half * SHARD:(half + 1) * SHARD]
        out = dot(one_hot(rel, step), term, 1, 1).astype(BF16)
        for quarter in range(4):
            rel_out[4 * step + quarter] = out[quarter * 64:(quarter + 1) * 64]


def early_terms(core, block, table):
    vmem = pl.BlockSpec(memory_space=pltpu.VMEM)
    return pl.pallas_call(
        early_kernel,
        out_shape=(jax.ShapeDtypeStruct((D, EDGES), F32), jax.ShapeDtypeStruct((PARTS, 128), F32)),
        in_specs=[pl.BlockSpec(memory_space=pltpu.SMEM)] + [vmem] * 2,
        out_specs=(vmem, vmem),
        compiler_params=pltpu.CompilerParams(vmem_limit_bytes=24 << 20),
        cost_estimate=pl.CostEstimate(flops=1 << 30, bytes_accessed=3 << 20, transcendentals=0),
    )(core, block, table)


def edge_terms(core, zh, block_a, block_b, w_a, w_b, counts_a, counts_b, mine, other):
    vmem = pl.BlockSpec(memory_space=pltpu.VMEM)
    block = jax.ShapeDtypeStruct((4, SHARD, D), BF16)
    return pl.pallas_call(
        edge_kernel,
        out_shape=(block, block, jax.ShapeDtypeStruct((16, 64, D), BF16)),
        in_specs=[pl.BlockSpec(memory_space=pltpu.SMEM)] * 2 + [vmem] * 8,
        out_specs=(vmem, vmem, vmem),
        compiler_params=pltpu.CompilerParams(vmem_limit_bytes=40 << 20),
    )(core, zh, block_a, block_b, w_a, w_b, counts_a, counts_b, mine, other)


def swap(block, axis, distance=1):
    size = lax.axis_size(axis)
    return lax.ppermute(block, axis, [(i, i ^ distance) for i in range(size)])


def spread(block, axis, size):
    copies = jnp.broadcast_to(block[None], (size,) + block.shape)
    return lax.all_to_all(copies, axis, 0, 0)


def summed(blocks):
    return jnp.sum(blocks.astype(F32), axis=0).astype(BF16)


def exchange(blocks, axis):
    return lax.all_to_all(blocks, axis, 0, 0)


def tie(*values):
    return lax.optimization_barrier(values)


def local(embeddings, relations, lhs_ids, rhs_ids, rel_ids, neg_ids, live):
    core = lax.axis_index("core").astype(jnp.int32)[None]
    zh = lax.axis_index("zh").astype(jnp.int32)[None]
    ids = pack_ids(lhs_ids[0, 0], rhs_ids[0, 0], rel_ids[0, 0], neg_ids[0, 0, 0], live)
    block_a = jnp.concatenate([embeddings, ids], axis=0)
    block_b = swap(block_a, "yh")
    w_a, counts_a = early_terms(core, block_a, relations)
    block_b, w_a, counts_a = tie(block_b, w_a, counts_a)
    both = jnp.concatenate([embeddings, block_b[:SHARD]], axis=0)
    mine = lax.all_gather(both, "zh", axis=0, tiled=False)
    other = swap(mine, "core")
    w_b, counts_b = early_terms(core, block_b, relations)
    mine_sum, other_sum, rel_part = edge_terms(
        core, zh, block_a, block_b, w_a, w_b, counts_a, counts_b, mine, other
    )
    from_core = swap(other_sum, "core")
    parts = exchange(rel_part, NEAR)
    chip = mine_sum.astype(F32) + from_core.astype(F32)
    far = swap(chip[2:], "zh", 2)
    parts = spread(summed(parts), FAR, 4)
    far, parts = tie(far, parts)
    pair = chip[:2] + far
    near = swap(pair[1].astype(BF16), "zh", 1)
    rel_all = spread(summed(parts), NEAR, 16).reshape(PARTS, D).astype(F32)
    near, rel_all = tie(near, rel_all)
    return pair[0] + near.astype(F32), rel_all


def solution(mesh):
    fine = Mesh(mesh.devices.reshape(2, 2, 2, 4, 2, 4, 2), AXES)
    dom, rel = AXES[:5], AXES[5:]
    placed = (
        P(AXES, None),
        P(rel, None),
        P(dom, rel, None),
        P(dom, rel, None),
        P(dom, rel, None),
        P(dom, rel, None, None),
        P(AXES),
    )
    return jax.shard_map(
        local,
        mesh=fine,
        in_specs=placed,
        out_specs=(P(AXES, None), P(rel, None)),
        check_vma=False,
    )
```
